256 devices in a mesh: head: 4 (over x), outer: 16 (over y, z_lo, core), inner: 4 (over z_hi).
Axes of the slice: x: 4, y: 4, z: 8 (z_hi: 4, z_lo: 2; z = z_hi * 2 + z_lo), core: 2. Of those that a mesh axis runs over, the one named last changes fastest.
Arguments:
- queries: bfloat16 [128, 128, 8192], P(('outer', 'inner'), 'head'), may hold values from -5 to 5
- keys: bfloat16 [128, 128, 1024], P(('outer', 'inner'), 'head'), may hold values from -5 to 5
- values: bfloat16 [128, 128, 1024], P(('outer', 'inner'), 'head'), may hold values from -6 to 6
- half_order: int32 [128], replicated, may hold values from 0 to 127, each once
- window: int32 [8], replicated, may hold values from 4 to 16, as said below
Outputs:
- attended: bfloat16 [128, 128, 8192], P(('outer', 'inner'), 'head')
The draws below stay inside these ranges and needn't reach their ends.
Inputs may be any that keep to these rules, and one draw needn't show every extreme that they name: `half_order`: a permutation of 0 to 127. Some key head has window 16.
All inputs are finite; a program needn't handle non-finite values.
Results may differ from the reference program's by a relative error of at most 0.0045.
Values may be sent and summed in bfloat16 or wider, within the bound.
A program may use at most 128 MiB of HBM per device.

```python
import math
import jax
import jax.numpy as jnp
from jax import lax

QH = 64
KVH = 8
HD = 128
HALF = 128
WIN = 16
HALVES = 128


def draw_queries(key, part):
    key = jax.random.fold_in(key, 11)
    base = jnp.clip(jax.random.normal(key, (HALVES, HALF, QH * HD), jnp.float32), -5.0, 5.0)
    return base.astype(jnp.bfloat16)


def draw_keys(key, part):
    key = jax.random.fold_in(key, 13)
    base = jnp.clip(jax.random.normal(key, (HALVES, HALF, KVH * HD), jnp.float32), -5.0, 5.0)
    return base.astype(jnp.bfloat16)


def draw_window(key, part):
    key = jax.random.fold_in(key, 17)
    width_key, index_key = jax.random.split(key)
    widths = jax.random.randint(width_key, (KVH,), WIN // 4, WIN + 1, dtype=jnp.int32)
    chosen = jax.random.randint(index_key, (), 0, KVH, dtype=jnp.int32)
    return jnp.where(jnp.arange(KVH, dtype=jnp.int32) == chosen, WIN, widths).astype(jnp.int32)


def block_scale(own_key, shape, cuts, smallest, top_value):
    gain = 1.0
    for position, blocks in cuts:
        steps = jax.random.uniform(jax.random.fold_in(jax.random.fold_in(own_key, 6), position), (blocks,), jnp.float32, smallest / len(cuts), top_value / len(cuts))
        gain = gain * jnp.repeat(jnp.exp(steps), shape[position] // blocks).reshape((-1,) + (1,) * (len(shape) - 1 - position))
    return gain


def normal_values(own_key, extent, width, bound, shards=(), held_as=jnp.bfloat16):
    gain = block_scale(own_key, extent, shards, -0.22, 0.18) if shards else 1.0
    values = jax.random.normal(own_key, extent, jnp.float32) * width * gain
    return jnp.minimum(jnp.maximum(values, -bound), bound).astype(held_as)


def setup_inputs(seed: int = 0) -> dict:
    key_list = jax.random.split(jax.random.key(seed), 6)
    queries = draw_queries(jax.random.fold_in(key_list[5], 71), 0)
    keys = draw_keys(jax.random.fold_in(key_list[5], 71), 0)
    values = normal_values(key_list[2], (HALVES, HALF, KVH * HD), 1.0, 6.0, ((0, 64), (1, 4)))
    half_order = jax.random.permutation(key_list[3], HALVES).astype(jnp.int32)
    window = draw_window(jax.random.fold_in(key_list[5], 71), 0)
    return {"queries": queries, "keys": keys, "values": values, "half_order": half_order, "window": window}


def reference(queries, keys, values, half_order, window):
    halves_all = queries.shape[0]
    half_rows = queries.shape[1]
    group_size = QH // KVH
    inverse = jnp.argsort(half_order).astype(jnp.int32)
    seq_queries = queries[inverse].reshape(halves_all, half_rows, KVH, group_size, HD)
    padding = jnp.zeros((WIN, half_rows, KVH * HD), jnp.bfloat16)
    pad_keys = jnp.concatenate([padding, keys[inverse]], 0)
    pad_values = jnp.concatenate([padding, values[inverse]], 0)
    row_index = jnp.arange(half_rows, dtype=jnp.int32)

    def one_block(block):
        key_slab = lax.dynamic_slice_in_dim(pad_keys, block + 1, WIN, 0).reshape(WIN * half_rows, KVH, HD).astype(jnp.float32)
        value_slab = lax.dynamic_slice_in_dim(pad_values, block + 1, WIN, 0).reshape(WIN * half_rows, KVH, HD).astype(jnp.float32)
        query_block = lax.dynamic_index_in_dim(seq_queries, block, 0, keepdims=False).astype(jnp.float32)
        key_blocks = block - WIN + 1 + jnp.arange(WIN * half_rows, dtype=jnp.int32) // half_rows
        key_pos = key_blocks * half_rows + jnp.tile(row_index, WIN)
        query_pos = block * half_rows + row_index
        scores = jnp.einsum('tgjd,sgd->gjts', query_block, key_slab) / math.sqrt(HD)
        later = (key_pos[None, :] <= query_pos[:, None]) & (key_blocks >= 0)[None, :]
        inside = (block - key_blocks)[None, :] < window[:, None]
        seen = later[None, None, :, :] & inside[:, None, None, :]
        masked = jnp.where(seen, scores, -1e+30)
        peak = lax.optimization_barrier(jnp.max(masked, axis=-1, keepdims=True))
        weights = jnp.where(seen, jnp.exp(scores - peak), 0.0)
        denominator = lax.optimization_barrier(jnp.sum(weights, axis=-1))
        rounded = lax.optimization_barrier(weights.astype(jnp.bfloat16)).astype(jnp.float32)
        numerator = jnp.einsum('gjts,sgd->tgjd', rounded, value_slab)
        result = numerator / jnp.transpose(denominator, (2, 0, 1))[..., None]
        return result.astype(jnp.bfloat16).reshape(half_rows, QH * HD)
    outputs = lax.map(one_block, jnp.arange(halves_all, dtype=jnp.int32))
    return outputs[half_order]
```

```python
import functools
import math

import jax
import jax.numpy as jnp
import numpy as np
from jax import lax
from jax.experimental import pallas as pl
from jax.experimental.pallas import tpu as pltpu
from jax.sharding import PartitionSpec as P

HD = 128
WIN = 16
ROWS = 128
GROUP = 8
LOG2E = 1.4426950408889634
REL = [(dx, dzl) for dzl in (0, 1) for dx in range(4)]
RING = (0, -1, 1, 2)
MESH = pl.DeviceIdType.MESH


def attend_block(b, idx_ref, vis_ref, qbuf, kv, obuf, kslab, vslab):
    diag = kv[idx_ref[b * WIN + WIN - 1], 0]
    first = jnp.broadcast_to(diag[0:1, :].astype(jnp.float32), (ROWS, HD)).astype(jnp.bfloat16)
    for k in range(WIN):
        slot = idx_ref[b * WIN + k]
        seen_f32 = jnp.full((ROWS, HD), vis_ref[b * WIN + k].astype(jnp.float32))
        seen, unseen = seen_f32.astype(jnp.bfloat16), (1.0 - seen_f32).astype(jnp.bfloat16)
        rows = pl.ds(k * ROWS, ROWS)
        keys = kv[slot, 0] * seen + first * unseen
        kslab[rows, 0:HD] = keys
        kslab[rows, HD : 2 * HD] = keys
        vslab[rows, 0:HD] = kv[slot, 1] * seen
        vslab[rows, HD : 2 * HD] = seen
    row = lax.broadcasted_iota(jnp.int32, (ROWS, ROWS), 0)
    col = lax.broadcasted_iota(jnp.int32, (ROWS, ROWS), 1)
    causal = jnp.concatenate([col <= row] * 2, 0)

    def pair(j, carry):
        lanes = pl.ds(pl.multiple_of(j * 2 * HD, 2 * HD), 2 * HD)
        q = qbuf[b, :, lanes]
        q = jnp.concatenate([q[:, :HD], q[:, HD:]], 0).astype(jnp.float32) * (LOG2E / math.sqrt(HD))
        high = q.astype(jnp.bfloat16)
        low = (q - high.astype(jnp.float32)).astype(jnp.bfloat16)
        s = lax.dot_general(
            jnp.concatenate([high, low], 1), kslab[...], (((1,), (1,)), ((), ())),
            preferred_element_type=jnp.float32,
        )
        edge = (WIN - 1) * ROWS
        s = jnp.concatenate([s[:, :edge], jnp.where(causal, s[:, edge:], -1e30)], 1)
        peak = jnp.max(s, axis=1, keepdims=True)
        p = jnp.exp2(s - peak).astype(jnp.bfloat16)
        o = jnp.dot(p, vslab[...], preferred_element_type=jnp.float32)
        r = (o[:, :HD] / o[:, HD:]).astype(jnp.bfloat16)
        obuf[b, :, lanes] = jnp.concatenate([r[:ROWS], r[ROWS:]], 1)
        return carry

    lax.fori_loop(0, GROUP // 2, pair, 0)


def kernel(idx_ref, vis_ref, q_ref, k_ref, v_ref, o_ref, qbuf, kv, obuf, kslab, vslab,
           a_send, a_recv, g_send, g_recv, o_send, o_recv, local):
    x = lax.axis_index("head")
    outer = lax.axis_index("outer")
    zh = lax.axis_index("inner")
    y, zl, c = outer // 4, (outer // 2) % 2, outer % 2

    def dev(dx=0, dy=0, dzl=0, dc=0, dzh=0):
        yy = (y + dy + 4) % 4
        ll = (zl + dzl) % 2
        cc = (c + dc) % 2
        return {"head": (x + dx + 4) % 4, "outer": yy * 4 + ll * 2 + cc, "inner": (zh + dzh + 4) % 4}

    def slot(dy=0, dzh=0, dc=0):
        return ((((y + dy + 4) % 4) * 4 + (zh + dzh + 4) % 4) * 2 + (c + dc) % 2) * 4

    barrier = pltpu.get_barrier_semaphore()
    partners = [dev(dx=dx, dzl=dzl) for dx, dzl in REL[1:]]
    partners += [dev(dzh=1), dev(dzh=-1), dev(dy=1), dev(dy=-1), dev(dc=1)]
    for partner in partners:
        pl.semaphore_signal(barrier, inc=1, device_id=partner, device_id_type=MESH)
    pl.semaphore_wait(barrier, len(partners))

    sent = []

    def exchange(src, width, dst, send, recv, here):
        arriving = []
        for n, (dx, dzl) in enumerate(REL):
            xx, ll = (x + dx) % 4, (zl + dzl) % 2
            lanes = pl.ds(pl.multiple_of((xx * 2 + ll) * width, width), width)
            if n == 0:
                copy = pltpu.make_async_copy(src.at[:, :, lanes], dst(x, zl), here)
                copy.start()
                arriving.append(copy.wait)
            else:
                copy = pltpu.make_async_remote_copy(
                    src.at[:, :, lanes], dst(x, zl), send.at[n], recv.at[n],
                    device_id=dev(dx=dx, dzl=dzl), device_id_type=MESH)
                copy.start()
                sent.append(copy)
                back = pltpu.make_async_remote_copy(
                    src.at[:, :, lanes], dst((x - dx + 4) % 4, ll), send.at[n], recv.at[n],
                    device_id=dev(dx=dx, dzl=dzl), device_id_type=MESH)
                arriving.append(back.wait_recv)
        return arriving

    own = slot()
    arriving = []
    for which, src in ((0, k_ref), (1, v_ref)):
        arriving += exchange(
            src, HD,
            lambda xx, ll, which=which: kv.at[pl.ds(own + 2 * ll, 2), which, pl.ds(32 * xx, 32), :],
            a_send.at[which], a_recv.at[which], local.at[which])
    queries_in = exchange(
        q_ref, GROUP * HD,
        lambda xx, ll: qbuf.at[pl.ds(2 * ll, 2), pl.ds(32 * xx, 32), :],
        a_send.at[2], a_recv.at[2], local.at[2])
    for wait in arriving:
        wait()

    names = {}

    def copy_of(name, first, count, device):
        n = names.setdefault(name, len(names))
        part = kv.at[pl.ds(first, count)]
        return pltpu.make_async_remote_copy(
            part, part, g_send.at[n], g_recv.at[n], device_id=device, device_id_type=MESH)

    def send(name, first, count, device):
        copy = copy_of(name, first, count, device)
        copy.start()
        sent.append(copy)

    def arrived(name, first, count):
        copy_of(name, first, count, dev(dc=1)).wait_recv()

    pending = []

    def share(name, dy, dzh, half=None):
        off, count = (0, 4) if half is None else (2 * half, 2)
        send(("c", name), slot(dy, dzh) + off, count, dev(dc=1))
        pending.append((("c", name), slot(dy, dzh, 1) + off, count))

    def along_y(r):
        send(("y+", r), slot(0, r), 4, dev(dy=1))
        send(("y-", r), slot(0, r), 4, dev(dy=-1))
        share((0, r), 0, r)

    def onward(r):
        arrived(("y+", r), slot(-1, r), 4)
        send(("yy+", r), slot(-1, r), 2, dev(dy=1))
        share((-1, r), -1, r)
        arrived(("y-", r), slot(1, r), 4)
        send(("yy-", r), slot(1, r) + 2, 2, dev(dy=-1))
        share((1, r), 1, r)

    def opposite(r):
        arrived(("yy+", r), slot(2, r), 2)
        share((2, r, 0), 2, r, 0)
        arrived(("yy-", r), slot(2, r) + 2, 2)
        share((2, r, 1), 2, r, 1)

    send("z+", slot(), 4, dev(dzh=1))
    send("z-", slot(), 4, dev(dzh=-1))
    along_y(0)
    arrived("z+", slot(0, -1), 4)
    send("zz+", slot(0, -1), 2, dev(dzh=1))
    along_y(-1)
    arrived("z-", slot(0, 1), 4)
    send("zz-", slot(0, 1) + 2, 2, dev(dzh=-1))
    along_y(1)
    onward(0)
    arrived("zz+", slot(0, 2), 2)
    arrived("zz-", slot(0, 2) + 2, 2)
    along_y(2)
    onward(-1)
    onward(1)
    opposite(0)
    onward(2)
    opposite(-1)
    opposite(1)
    opposite(2)
    for wait in queries_in:
        wait()
    for item in pending:
        arrived(*item)

    head = x * 2 + zl
    lanes = pl.ds(pl.multiple_of(head * GROUP * HD, GROUP * HD), GROUP * HD)

    def returns(dzl, i, start):
        b = 2 * ((zl + dzl) % 2) + i
        for dx in range(4):
            xx = (x + dx) % 4
            src = obuf.at[b, pl.ds(32 * xx, 32), :]
            if dx == 0 and dzl == 0:
                copy = pltpu.make_async_copy(src, o_ref.at[i, :, lanes], local.at[3 + i])
                copy.start() if start else copy.wait()
                continue
            n = dzl * 4 + dx
            copy = pltpu.make_async_remote_copy(
                src, o_ref.at[i, :, lanes], o_send.at[n, i], o_recv.at[n, i],
                device_id=dev(dx=dx, dzl=dzl), device_id_type=MESH)
            if start:
                copy.start()
            else:
                copy.wait_send()
                from_head = ((x - dx + 4) % 4) * 2 + (zl + dzl) % 2
                there = pl.ds(pl.multiple_of(from_head * GROUP * HD, GROUP * HD), GROUP * HD)
                pltpu.make_async_remote_copy(
                    src, o_ref.at[i, :, there], o_send.at[n, i], o_recv.at[n, i],
                    device_id=dev(dx=dx, dzl=dzl), device_id_type=MESH).wait_recv()

    for dzl in (1, 0):
        for i in range(2):
            b = 2 * ((zl + dzl) % 2) + i
            attend_block(b, idx_ref, vis_ref, qbuf, kv, obuf, kslab, vslab)
            returns(dzl, i, True)
    for copy in sent:
        copy.wait_send()
    for dzl in (1, 0):
        for i in range(2):
            returns(dzl, i, False)


def body(queries, keys, values, half_order, window):
    x = lax.axis_index("head")
    outer = lax.axis_index("outer")
    zh = lax.axis_index("inner")
    y, zl, c = outer // 4, (outer // 2) % 2, outer % 2
    slots = np.arange(128).reshape(4, 4, 2, 2, 2).transpose(0, 3, 2, 1, 4).reshape(128).astype(np.int32)
    place = jnp.sum(jnp.where(half_order[:, None] == jnp.arange(128)[None, :], slots[:, None], 0), 0)
    mine = ((y * 4 + np.repeat(np.arange(2), 2) * 2 + c) * 4 + zh) * 2 + np.tile(np.arange(2), 2)
    wanted = half_order[mine][:, None] + jnp.arange(1 - WIN, 1, dtype=jnp.int32)[None, :]
    back = WIN - 1 - jnp.arange(WIN, dtype=jnp.int32)[None, :]
    vis = ((wanted >= 0) & (back < window[x * 2 + zl])).astype(jnp.int32)
    idx = place[jnp.maximum(wanted, 0)]
    smem = pl.BlockSpec(memory_space=pltpu.SMEM)
    hbm = pl.BlockSpec(memory_space=pl.ANY)
    dma = pltpu.SemaphoreType.DMA
    return pl.pallas_call(
        kernel,
        out_shape=jax.ShapeDtypeStruct(queries.shape, jnp.bfloat16),
        in_specs=[smem, smem, hbm, hbm, hbm],
        out_specs=hbm,
        scratch_shapes=[
            pltpu.VMEM((4, ROWS, GROUP * HD), jnp.bfloat16),
            pltpu.VMEM((128, 2, ROWS, HD), jnp.bfloat16),
            pltpu.VMEM((4, ROWS, GROUP * HD), jnp.bfloat16),
            pltpu.VMEM((WIN * ROWS, 2 * HD), jnp.bfloat16),
            pltpu.VMEM((WIN * ROWS, 2 * HD), jnp.bfloat16),
            dma((3, 8)), dma((3, 8)),
            dma((48,)), dma((48,)),
            dma((8, 2)), dma((8, 2)),
            dma((5,)),
        ],
        compiler_params=pltpu.CompilerParams(
            collective_id=0, has_side_effects=True, vmem_limit_bytes=48 * 1024 * 1024),
    )(idx.reshape(-1), vis.reshape(-1), queries, keys, values)


def solution(mesh):
    rows = P(("outer", "inner"), "head", None)
    return jax.shard_map(
        body,
        mesh=mesh,
        in_specs=(rows, rows, rows, P(), P()),
        out_specs=rows,
        check_vma=False,
    )
```

```python
import math

import jax
import jax.numpy as jnp
from jax import lax
from jax.experimental import pallas as pl
from jax.experimental.pallas import tpu as pltpu
from jax.sharding import PartitionSpec as P

HD = 128
WIN = 16
ROWS = 128
GROUP = 8
LOG2E = 1.4426950408889634
REL = [(dx, dzl) for dzl in (0, 1) for dx in range(4)]
RING = (0, -1, 1, 2)
MESH = pl.DeviceIdType.MESH


def slot_at(table, n):
    return jnp.clip(table[0, n], 0, 127)


def attend_block(b, table, qbuf, kv, obuf, kslab, vslab):
    diag = kv[slot_at(table, b * WIN + WIN - 1), 0]
    first = jnp.broadcast_to(diag[0:1, :].astype(jnp.float32), (ROWS, HD)).astype(jnp.bfloat16)
    for k in range(WIN):
        slot = slot_at(table, b * WIN + k)
        seen_f32 = jnp.full((ROWS, HD), table[1, b * WIN + k].astype(jnp.float32))
        seen, unseen = seen_f32.astype(jnp.bfloat16), (1.0 - seen_f32).astype(jnp.bfloat16)
        rows = pl.ds(k * ROWS, ROWS)
        keys = kv[slot, 0] * seen + first * unseen
        kslab[rows, 0:HD] = keys
        kslab[rows, HD : 2 * HD] = keys
        vslab[rows, 0:HD] = kv[slot, 1] * seen
        vslab[rows, HD : 2 * HD] = seen
    row = lax.broadcasted_iota(jnp.int32, (ROWS, ROWS), 0)
    col = lax.broadcasted_iota(jnp.int32, (ROWS, ROWS), 1)
    causal = jnp.concatenate([col <= row] * 2, 0)

    for j in range(GROUP // 2):
        lanes = slice(j * 2 * HD, (j + 1) * 2 * HD)
        q = qbuf[b, :, lanes]
        q = jnp.concatenate([q[:, :HD], q[:, HD:]], 0).astype(jnp.float32) * (LOG2E / math.sqrt(HD))
        high = q.astype(jnp.bfloat16)
        low = (q - high.astype(jnp.float32)).astype(jnp.bfloat16)
        s = lax.dot_general(
            jnp.concatenate([high, low], 1), kslab[...], (((1,), (1,)), ((), ())),
            preferred_element_type=jnp.float32,
        )
        edge = (WIN - 1) * ROWS
        s = jnp.concatenate([s[:, :edge], jnp.where(causal, s[:, edge:], -1e30)], 1)
        peak = jnp.max(s, axis=1, keepdims=True)
        p = jnp.exp2(s - peak).astype(jnp.bfloat16)
        o = jnp.dot(p, vslab[...], preferred_element_type=jnp.float32)
        r = (o[:, :HD] / o[:, HD:]).astype(jnp.bfloat16)
        obuf[b, :, lanes] = jnp.concatenate([r[:ROWS], r[ROWS:]], 1)


def kernel(order_ref, window_ref, row_ref, q_ref, k_ref, v_ref, o_ref, qbuf, kv, obuf, kslab, vslab, lookup, table,
           a_send, a_recv, g_send, g_recv, o_send, o_recv, local):
    x = lax.axis_index("head")
    outer = lax.axis_index("outer")
    zh = lax.axis_index("inner")
    y, zl, c = outer // 4, (outer // 2) % 2, outer % 2

    def dev(dx=0, dy=0, dzl=0, dc=0, dzh=0):
        yy = (y + dy + 4) % 4
        ll = (zl + dzl) % 2
        cc = (c + dc) % 2
        return {"head": (x + dx + 4) % 4, "outer": yy * 4 + ll * 2 + cc, "inner": (zh + dzh + 4) % 4}

    def slot(dy=0, dzh=0, dc=0):
        return ((((y + dy + 4) % 4) * 4 + (zh + dzh + 4) % 4) * 2 + (c + dc) % 2) * 4

    barrier = pltpu.get_barrier_semaphore()
    partners = [dev(dx=dx, dzl=dzl) for dx, dzl in REL[1:]]
    partners += [dev(dzh=1), dev(dzh=-1), dev(dy=1), dev(dy=-1), dev(dc=1)]
    for partner in partners:
        pl.semaphore_signal(barrier, inc=1, device_id=partner, device_id_type=MESH)
    pl.semaphore_wait(barrier, len(partners))

    sent = []

    def exchange(src, width, dst, send, recv, here):
        arriving = []
        for n, (dx, dzl) in enumerate(REL):
            xx, ll = (x + dx) % 4, (zl + dzl) % 2
            lanes = pl.ds(pl.multiple_of((xx * 2 + ll) * width, width), width)
            if n == 0:
                copy = pltpu.make_async_copy(src.at[:, :, lanes], dst(x, zl), here)
                copy.start()
                arriving.append(copy.wait)
            else:
                copy = pltpu.make_async_remote_copy(
                    src.at[:, :, lanes], dst(x, zl), send.at[n], recv.at[n],
                    device_id=dev(dx=dx, dzl=dzl), device_id_type=MESH)
                copy.start()
                sent.append(copy)
                back = pltpu.make_async_remote_copy(
                    src.at[:, :, lanes], dst((x - dx + 4) % 4, ll), send.at[n], recv.at[n],
                    device_id=dev(dx=dx, dzl=dzl), device_id_type=MESH)
                arriving.append(back.wait_recv)
        return arriving

    own = slot()
    arriving = []
    for which, src in ((0, k_ref), (1, v_ref)):
        arriving += exchange(
            src, HD,
            lambda xx, ll, which=which: kv.at[pl.ds(own + 2 * ll, 2), which, pl.ds(32 * xx, 32), :],
            a_send.at[which], a_recv.at[which], local.at[which])
    lane = lax.broadcasted_iota(jnp.int32, (1, ROWS), 1)
    block = jnp.zeros((1, ROWS), jnp.int32)
    for b in range(4):
        stored = ((y * 4 + b // 2 * 2 + c) * 4 + zh) * 2 + b % 2
        block = jnp.where(lane // WIN == b, order_ref[stored], block)
    back = WIN - 1 - lane % WIN
    wanted = block - back
    j = lax.broadcasted_iota(jnp.int32, (ROWS, ROWS), 0)
    slots = (((j // 32) * 4 + (j // 2) % 4) * 2 + (j // 8) % 2) * 4 + (j // 16) % 2 * 2 + j % 2
    order = jnp.broadcast_to(row_ref[...], (ROWS, ROWS)).T
    lookup[0:1, :] = jnp.sum(jnp.where(order == wanted, slots, 0), axis=0, keepdims=True)
    lookup[1:2, :] = ((wanted >= 0) & (back < window_ref[x * 2 + zl])).astype(jnp.int32)
    lookup[2:8, :] = jnp.zeros((6, ROWS), jnp.int32)
    listing = pltpu.make_async_copy(lookup, table, local.at[5])
    listing.start()
    for wait in arriving:
        wait()

    names = {}

    def copy_of(name, first, count, device):
        n = names.setdefault(name, len(names))
        part = kv.at[pl.ds(first, count)]
        return pltpu.make_async_remote_copy(
            part, part, g_send.at[n], g_recv.at[n], device_id=device, device_id_type=MESH)

    def send(name, first, count, device):
        copy = copy_of(name, first, count, device)
        copy.start()
        sent.append(copy)

    def arrived(name, first, count):
        copy_of(name, first, count, dev(dc=1)).wait_recv()

    pending = []

    def share(name, dy, dzh, half=None):
        off, count = (0, 4) if half is None else (2 * half, 2)
        send(("c", name), slot(dy, dzh) + off, count, dev(dc=1))
        pending.append((("c", name), slot(dy, dzh, 1) + off, count))

    def along_y(r, h):
        send(("y+", r, h), slot(0, r) + 2 * h, 2, dev(dy=1))
        send(("y-", r, h), slot(0, r) + 2 * h, 2, dev(dy=-1))

    def from_y(r, h, down):
        dy = 1 if down else -1
        arrived(("y-" if down else "y+", r, h), slot(dy, r) + 2 * h, 2)
        if down == (h == 1):
            send(("yy", r, down), slot(dy, r) + 2 * h, 2, dev(dy=-dy))

    def opposite(r):
        arrived(("yy", r, False), slot(2, r), 2)
        share((2, r, 0), 2, r, 0)
        arrived(("yy", r, True), slot(2, r) + 2, 2)
        share((2, r, 1), 2, r, 1)

    def z(h, down):
        send(("z", down, h), slot() + 2 * h, 2, dev(dzh=-1 if down else 1))

    def from_z(h, down):
        r = 1 if down else -1
        arrived(("z", down, h), slot(0, r) + 2 * h, 2)
        if down == (h == 1):
            send(("zz", down), slot(0, r) + 2 * h, 2, dev(dzh=-r))

    z(0, False)
    z(1, True)
    along_y(0, 0)
    along_y(0, 1)
    z(1, False)
    z(0, True)
    share((0, 0), 0, 0)
    from_z(0, False)
    along_y(-1, 0)
    from_z(1, True)
    along_y(1, 1)
    from_y(0, 0, False)
    from_y(0, 1, True)
    from_z(1, False)
    along_y(-1, 1)
    from_z(0, True)
    along_y(1, 0)
    share((0, -1), 0, -1)
    share((0, 1), 0, 1)
    queries_in = exchange(
        q_ref, GROUP * HD,
        lambda xx, ll: qbuf.at[pl.ds(2 * ll, 2), pl.ds(32 * xx, 32), :],
        a_send.at[2], a_recv.at[2], local.at[2])
    from_y(0, 1, False)
    share((-1, 0), -1, 0)
    from_y(0, 0, True)
    share((1, 0), 1, 0)
    arrived(("zz", False), slot(0, 2), 2)
    along_y(2, 0)
    arrived(("zz", True), slot(0, 2) + 2, 2)
    along_y(2, 1)
    share((0, 2), 0, 2)
    for r in (-1, 1):
        from_y(r, 0, False)
        from_y(r, 1, True)
    opposite(0)
    for r in (-1, 1):
        from_y(r, 1, False)
        share((-1, r), -1, r)
        from_y(r, 0, True)
        share((1, r), 1, r)
    from_y(2, 0, False)
    from_y(2, 1, True)
    opposite(-1)
    opposite(1)
    from_y(2, 1, False)
    share((-1, 2), -1, 2)
    from_y(2, 0, True)
    share((1, 2), 1, 2)
    opposite(2)
    listing.wait()
    for wait in queries_in:
        wait()
    for item in pending:
        arrived(*item)

    head = x * 2 + zl
    lanes = pl.ds(pl.multiple_of(head * GROUP * HD, GROUP * HD), GROUP * HD)

    def returns(dzl, i, start):
        b = 2 * ((zl + dzl) % 2) + i
        for dx in range(4):
            xx = (x + dx) % 4
            src = obuf.at[b, pl.ds(32 * xx, 32), :]
            if dx == 0 and dzl == 0:
                copy = pltpu.make_async_copy(src, o_ref.at[i, :, lanes], local.at[3 + i])
                copy.start() if start else copy.wait()
                continue
            n = dzl * 4 + dx
            copy = pltpu.make_async_remote_copy(
                src, o_ref.at[i, :, lanes], o_send.at[n, i], o_recv.at[n, i],
                device_id=dev(dx=dx, dzl=dzl), device_id_type=MESH)
            if start:
                copy.start()
            else:
                copy.wait_send()
                from_head = ((x - dx + 4) % 4) * 2 + (zl + dzl) % 2
                there = pl.ds(pl.multiple_of(from_head * GROUP * HD, GROUP * HD), GROUP * HD)
                pltpu.make_async_remote_copy(
                    src, o_ref.at[i, :, there], o_send.at[n, i], o_recv.at[n, i],
                    device_id=dev(dx=dx, dzl=dzl), device_id_type=MESH).wait_recv()

    for dzl in (1, 0):
        for i in range(2):
            b = 2 * ((zl + dzl) % 2) + i
            attend_block(b, table, qbuf, kv, obuf, kslab, vslab)
            returns(dzl, i, True)
    for copy in sent:
        copy.wait_send()
    for dzl in (1, 0):
        for i in range(2):
            returns(dzl, i, False)


def body(queries, keys, values, half_order, window):
    smem = pl.BlockSpec(memory_space=pltpu.SMEM)
    hbm = pl.BlockSpec(memory_space=pl.ANY)
    dma = pltpu.SemaphoreType.DMA
    return pl.pallas_call(
        kernel,
        out_shape=jax.ShapeDtypeStruct(queries.shape, jnp.bfloat16),
        in_specs=[smem, smem, pl.BlockSpec(memory_space=pltpu.VMEM), hbm, hbm, hbm],
        out_specs=hbm,
        scratch_shapes=[
            pltpu.VMEM((4, ROWS, GROUP * HD), jnp.bfloat16),
            pltpu.VMEM((128, 2, ROWS, HD), jnp.bfloat16),
            pltpu.VMEM((4, ROWS, GROUP * HD), jnp.bfloat16),
            pltpu.VMEM((WIN * ROWS, 2 * HD), jnp.bfloat16),
            pltpu.VMEM((WIN * ROWS, 2 * HD), jnp.bfloat16),
            pltpu.VMEM((8, ROWS), jnp.int32),
            pltpu.SMEM((8, ROWS), jnp.int32),
            dma((3, 8)), dma((3, 8)),
            dma((80,)), dma((80,)),
            dma((8, 2)), dma((8, 2)),
            dma((6,)),
        ],
        compiler_params=pltpu.CompilerParams(
            collective_id=0, has_side_effects=True, vmem_limit_bytes=48 * 1024 * 1024),
    )(half_order, window, half_order.reshape(1, ROWS), queries, keys, values)


def solution(mesh):
    rows = P(("outer", "inner"), "head", None)
    return jax.shard_map(
        body,
        mesh=mesh,
        in_specs=(rows, rows, rows, P(), P()),
        out_specs=rows,
        check_vma=False,
    )
```

```python
import math

import jax
import jax.numpy as jnp
from jax import lax
from jax.experimental import pallas as pl
from jax.experimental.pallas import tpu as pltpu
from jax.sharding import PartitionSpec as P

HD = 128
WIN = 16
ROWS = 128
GROUP = 8
LOG2E = 1.4426950408889634
TILE = 2
VTILE = 2
REL = [(dx, dzl) for dzl in (0, 1) for dx in range(4)]
RING = (0, -1, 1, 2)
MESH = pl.DeviceIdType.MESH


def slot_at(table, n):
    return jnp.clip(table[0, n], 0, 127)


def key_slab(b, table, kbuf, kslab):
    first = kbuf[slot_at(table, b * WIN + WIN - 1)][0:1, :].astype(jnp.float32)
    first = jnp.broadcast_to(first, (ROWS, HD)).astype(jnp.bfloat16)
    for k in range(WIN):
        seen = jnp.full((ROWS, HD), table[1, b * WIN + k].astype(jnp.float32))
        unseen = (1.0 - seen).astype(jnp.bfloat16)
        keys = kbuf[slot_at(table, b * WIN + k)] * seen.astype(jnp.bfloat16) + first * unseen
        kslab[k * ROWS : (k + 1) * ROWS, 0:HD] = keys
        kslab[k * ROWS : (k + 1) * ROWS, HD : 2 * HD] = keys


def value_slab(b, table, vbuf, vslab):
    for k in range(WIN):
        seen = jnp.full((ROWS, HD), table[1, b * WIN + k].astype(jnp.float32)).astype(jnp.bfloat16)
        vslab[k * ROWS : (k + 1) * ROWS, 0:HD] = vbuf[slot_at(table, b * WIN + k)] * seen
        vslab[k * ROWS : (k + 1) * ROWS, HD : 2 * HD] = seen


def scores(b, j, qbuf, kslab, weights):
    row = lax.broadcasted_iota(jnp.int32, (ROWS, ROWS), 0)
    col = lax.broadcasted_iota(jnp.int32, (ROWS, ROWS), 1)
    causal = jnp.concatenate([col <= row] * TILE, 0)
    for t in range(GROUP // 2 // TILE):
        first = (j * (GROUP // 2) + t * TILE) * HD
        q = qbuf[b, :, first : first + TILE * HD]
        q = jnp.concatenate([q[:, i * HD : (i + 1) * HD] for i in range(TILE)], 0)
        q = q.astype(jnp.float32) * (LOG2E / math.sqrt(HD))
        high = q.astype(jnp.bfloat16)
        low = (q - high.astype(jnp.float32)).astype(jnp.bfloat16)
        s = lax.dot_general(
            jnp.concatenate([high, low], 1), kslab[...], (((1,), (1,)), ((), ())),
            preferred_element_type=jnp.float32,
        )
        edge = (WIN - 1) * ROWS
        s = jnp.concatenate([s[:, :edge], jnp.where(causal, s[:, edge:], -1e30)], 1)
        peak = jnp.max(s, axis=1, keepdims=True)
        weights[t * TILE * ROWS : (t + 1) * TILE * ROWS, :] = jnp.exp2(s - peak).astype(jnp.bfloat16)


def sums(b, j, weights, vslab, obuf):
    for t in range(GROUP // 2 // VTILE):
        o = jnp.dot(weights[t * VTILE * ROWS : (t + 1) * VTILE * ROWS, :], vslab[...], preferred_element_type=jnp.float32)
        r = (o[:, :HD] / o[:, HD:]).astype(jnp.bfloat16)
        for i in range(VTILE):
            first = (j * (GROUP // 2) + t * VTILE + i) * HD
            obuf[b, :, first : first + HD] = r[i * ROWS : (i + 1) * ROWS]


def kernel(order_hbm, window_hbm, row_hbm, q_ref, k_ref, v_ref, o_ref, qbuf, kbuf, vbuf, obuf, weights0, weights1, kslab, vslab, lookup, table, order_ref, window_ref, row_ref,
           a_send, a_recv, g_send, g_recv, o_send, o_recv, local):
    x = lax.axis_index("head")
    outer = lax.axis_index("outer")
    zh = lax.axis_index("inner")
    y, zl, c = outer // 4, (outer // 2) % 2, outer % 2

    def dev(dx=0, dy=0, dzl=0, dc=0, dzh=0):
        yy = (y + dy + 4) % 4
        ll = (zl + dzl) % 2
        cc = (c + dc) % 2
        return {"head": (x + dx + 4) % 4, "outer": yy * 4 + ll * 2 + cc, "inner": (zh + dzh + 4) % 4}

    def slot(dy=0, dzh=0, dc=0):
        return ((((y + dy + 4) % 4) * 4 + (zh + dzh + 4) % 4) * 2 + (c + dc) % 2) * 4

    small = [pltpu.make_async_copy(src, dst, local.at[6 + n]) for n, (src, dst) in enumerate(
        ((order_hbm, order_ref), (window_hbm, window_ref), (row_hbm, row_ref)))]
    for copy in small:
        copy.start()
    barrier = pltpu.get_barrier_semaphore()
    partners = [dev(dx=dx, dzl=dzl) for dx, dzl in REL[1:]]
    partners += [dev(dzh=1), dev(dzh=-1), dev(dy=1), dev(dy=-1), dev(dc=1)]
    for partner in partners:
        pl.semaphore_signal(barrier, inc=1, device_id=partner, device_id_type=MESH)
    pl.semaphore_wait(barrier, len(partners))

    sent = []

    def exchange(src, width, dst, send, recv, here):
        arriving = []
        for n, (dx, dzl) in enumerate(REL):
            xx, ll = (x + dx) % 4, (zl + dzl) % 2
            lanes = pl.ds(pl.multiple_of((xx * 2 + ll) * width, width), width)
            if n == 0:
                copy = pltpu.make_async_copy(src.at[:, :, lanes], dst(x, zl, dzl), here)
                copy.start()
                arriving.append(copy.wait)
            else:
                copy = pltpu.make_async_remote_copy(
                    src.at[:, :, lanes], dst(x, zl, dzl), send.at[n], recv.at[n],
                    device_id=dev(dx=dx, dzl=dzl), device_id_type=MESH)
                copy.start()
                sent.append(copy)
                back = pltpu.make_async_remote_copy(
                    src.at[:, :, lanes], dst((x - dx + 4) % 4, ll, dzl), send.at[n], recv.at[n],
                    device_id=dev(dx=dx, dzl=dzl), device_id_type=MESH)
                arriving.append(back.wait_recv)
        return arriving

    own = slot()
    arriving = []
    bufs = (kbuf, vbuf)
    for which, src, buf in ((0, k_ref, kbuf), (1, v_ref, vbuf)):
        arriving += exchange(
            src, HD,
            lambda xx, ll, dzl, buf=buf: buf.at[pl.ds(own + 2 * ll, 2), pl.ds(32 * xx, 32), :],
            a_send.at[which], a_recv.at[which], local.at[which])
    for copy in small:
        copy.wait()
    lane = lax.broadcasted_iota(jnp.int32, (1, ROWS), 1)
    block = jnp.zeros((1, ROWS), jnp.int32)
    for b in range(4):
        stored = ((y * 4 + (zl + b // 2) % 2 * 2 + c) * 4 + zh) * 2 + b % 2
        block = jnp.where(lane // WIN == b, order_ref[stored], block)
    back = WIN - 1 - lane % WIN
    wanted = block - back
    j = lax.broadcasted_iota(jnp.int32, (ROWS, ROWS), 0)
    slots = (((j // 32) * 4 + (j // 2) % 4) * 2 + (j // 8) % 2) * 4 + (j // 16) % 2 * 2 + j % 2
    order = jnp.broadcast_to(row_ref[...], (ROWS, ROWS)).T
    lookup[0:1, :] = jnp.sum(jnp.where(order == wanted, slots, 0), axis=0, keepdims=True)
    lookup[1:2, :] = ((wanted >= 0) & (back < window_ref[x * 2 + zl])).astype(jnp.int32)
    lookup[2:8, :] = jnp.zeros((6, ROWS), jnp.int32)
    listing = pltpu.make_async_copy(lookup, table, local.at[5])
    listing.start()
    for wait in arriving[:8]:
        wait()

    names = {}

    def copy_of(name, w, first, count, device):
        n = names.setdefault((name, w), len(names))
        part = bufs[w].at[pl.ds(first, count)]
        return pltpu.make_async_remote_copy(
            part, part, g_send.at[n], g_recv.at[n], device_id=device, device_id_type=MESH)

    def send(name, w, first, count, device):
        copy = copy_of(name, w, first, count, device)
        copy.start()
        sent.append(copy)

    def arrived(name, w, first, count):
        copy_of(name, w, first, count, dev(dc=1)).wait_recv()

    pending = ([], [])

    def share(w, dy, dzh, half=None):
        off, count = (0, 4) if half is None else (2 * half, 2)
        name = ("c", dy, dzh, half)
        send(name, w, slot(dy, dzh) + off, count, dev(dc=1))
        pending[w].append((name, w, slot(dy, dzh, 1) + off, count))

    def to_z(w):
        send("z+", w, slot(), 4, dev(dzh=1))
        send("z-", w, slot(), 4, dev(dzh=-1))

    def from_z(w, r):
        arrived("z+" if r < 0 else "z-", w, slot(0, r), 4)
        half = 0 if r < 0 else 2
        send(("zz", r), w, slot(0, r) + half, 2, dev(dzh=-r))

    def from_zz(w):
        arrived(("zz", -1), w, slot(0, 2), 2)
        arrived(("zz", 1), w, slot(0, 2) + 2, 2)

    def to_y(w, r):
        send(("y+", r), w, slot(0, r), 4, dev(dy=1))
        send(("y-", r), w, slot(0, r), 4, dev(dy=-1))

    def from_y(w, r):
        arrived(("y+", r), w, slot(-1, r), 4)
        send(("yy+", r), w, slot(-1, r), 2, dev(dy=1))
        arrived(("y-", r), w, slot(1, r), 4)
        send(("yy-", r), w, slot(1, r) + 2, 2, dev(dy=-1))

    def share_y(w, r):
        share(w, -1, r)
        share(w, 1, r)

    def opposite(w, r):
        arrived(("yy+", r), w, slot(2, r), 2)
        share(w, 2, r, 0)
        arrived(("yy-", r), w, slot(2, r) + 2, 2)
        share(w, 2, r, 1)

    K, V = 0, 1
    to_z(K)
    to_y(K, 0)
    for wait in arriving[8:]:
        wait()
    to_z(V)
    to_y(V, 0)
    share(K, 0, 0)
    share(V, 0, 0)
    from_y(K, 0)
    from_z(K, -1)
    to_y(K, -1)
    from_z(K, 1)
    to_y(K, 1)
    from_y(V, 0)
    share(K, 0, -1)
    share(K, 0, 1)
    share_y(K, 0)
    from_z(V, -1)
    to_y(V, -1)
    from_z(V, 1)
    to_y(V, 1)
    from_zz(K)
    to_y(K, 2)
    queries_in = exchange(
        q_ref, GROUP * HD,
        lambda xx, ll, dzl: qbuf.at[pl.ds(2 * dzl, 2), pl.ds(32 * xx, 32), :],
        a_send.at[2], a_recv.at[2], local.at[2])
    from_y(K, -1)
    from_y(K, 1)
    share(K, 0, 2)
    share_y(K, -1)
    share_y(K, 1)
    from_zz(V)
    to_y(V, 2)
    opposite(K, 0)
    from_y(K, 2)
    share_y(K, 2)
    for r in (-1, 1, 2):
        share(V, 0, r)
    share_y(V, 0)
    from_y(V, -1)
    from_y(V, 1)
    for r in (-1, 1, 2):
        opposite(K, r)
    from_y(V, 2)
    share_y(V, -1)
    share_y(V, 1)
    opposite(V, 0)
    share_y(V, 2)
    opposite(V, -1)
    opposite(V, 1)
    opposite(V, 2)
    listing.wait()
    for wait in queries_in:
        wait()
    for item in pending[K]:
        arrived(*item)
    width = GROUP * HD // 2

    def returns(b, j, start):
        dzl, i = b // 2, b % 2
        part = slice(j * width, (j + 1) * width)

        def copy_to(dx, xx, ll):
            lanes = pl.ds(pl.multiple_of((xx * 2 + ll) * 2 * width + j * width, width), width)
            return pltpu.make_async_remote_copy(
                obuf.at[b, pl.ds(32 * ((x + dx) % 4), 32), part], o_ref.at[i, :, lanes],
                o_send.at[b, dx, j], o_recv.at[b, dx, j], device_id=dev(dx=dx, dzl=dzl), device_id_type=MESH)

        def remote(dx):
            if start:
                copy_to(dx, x, zl).start()
            else:
                copy_to(dx, x, zl).wait_send()
                copy_to(dx, (x - dx + 4) % 4, (zl + dzl) % 2).wait_recv()

        def here():
            lanes = pl.ds(pl.multiple_of((x * 2 + zl) * 2 * width + j * width, width), width)
            copy = pltpu.make_async_copy(
                obuf.at[b, pl.ds(32 * x, 32), part], o_ref.at[i, :, lanes], local.at[9 + 2 * i + j])
            copy.start() if start else copy.wait()

        for dx in (2, 1, 3):
            remote(dx)
        pl.when(dzl == 1)(lambda: remote(0))
        pl.when(dzl == 0)(here)

    def attend(n, last):
        b, after = (n + 2) % 4, (n + 3) % 4
        value_slab(b, table, vbuf, vslab)
        sums(b, 0, weights0, vslab, obuf)
        scores(b, 1, qbuf, kslab, weights1)
        returns(b, 0, True)
        sums(b, 1, weights1, vslab, obuf)
        if not last:
            key_slab(after, table, kbuf, kslab)
            scores(after, 0, qbuf, kslab, weights0)
        returns(b, 1, True)

    def attend_step(n, carry):
        attend(n, False)
        return carry

    def return_step(n, carry):
        returns((n + 2) % 4, 0, False)
        returns((n + 2) % 4, 1, False)
        return carry

    key_slab(2, table, kbuf, kslab)
    scores(2, 0, qbuf, kslab, weights0)
    for item in pending[V]:
        arrived(*item)
    lax.fori_loop(0, 3, attend_step, 0)
    attend(jnp.int32(3), True)
    for copy in sent:
        copy.wait_send()
    lax.fori_loop(0, 4, return_step, 0)


def body(queries, keys, values, half_order, window):
    hbm = pl.BlockSpec(memory_space=pltpu.HBM)
    dma = pltpu.SemaphoreType.DMA
    return pl.pallas_call(
        kernel,
        out_shape=jax.ShapeDtypeStruct(queries.shape, jnp.bfloat16),
        in_specs=[hbm] * 6,
        out_specs=hbm,
        scratch_shapes=[
            pltpu.VMEM((4, ROWS, GROUP * HD), jnp.bfloat16),
            pltpu.VMEM((128, ROWS, HD), jnp.bfloat16),
            pltpu.VMEM((128, ROWS, HD), jnp.bfloat16),
            pltpu.VMEM((4, ROWS, GROUP * HD), jnp.bfloat16),
            pltpu.VMEM((GROUP // 2 * ROWS, WIN * ROWS), jnp.bfloat16),
            pltpu.VMEM((GROUP // 2 * ROWS, WIN * ROWS), jnp.bfloat16),
            pltpu.VMEM((WIN * ROWS, 2 * HD), jnp.bfloat16),
            pltpu.VMEM((WIN * ROWS, 2 * HD), jnp.bfloat16),
            pltpu.VMEM((8, ROWS), jnp.int32),
            pltpu.SMEM((8, ROWS), jnp.int32),
            pltpu.SMEM((ROWS,), jnp.int32),
            pltpu.SMEM((8,), jnp.int32),
            pltpu.VMEM((1, ROWS), jnp.int32),
            dma((3, 8)), dma((3, 8)),
            dma((80,)), dma((80,)),
            dma((4, 4, 2)), dma((4, 4, 2)),
            dma((13,)),
        ],
        compiler_params=pltpu.CompilerParams(
            collective_id=0, has_side_effects=True, vmem_limit_bytes=60 * 1024 * 1024),
    )(half_order, window, half_order.reshape(1, ROWS), queries, keys, values)


def solution(mesh):
    rows = P(("outer", "inner"), "head", None)
    return jax.shard_map(
        body,
        mesh=mesh,
        in_specs=(rows, rows, rows, P(), P()),
        out_specs=rows,
        check_vma=False,
    )
```

```python
import math

import jax
import jax.numpy as jnp
from jax import lax
from jax.experimental import pallas as pl
from jax.experimental.pallas import tpu as pltpu
from jax.sharding import PartitionSpec as P

HD = 128
WIN = 16
ROWS = 128
GROUP = 8
LOG2E = 1.4426950408889634
TILE = 2
VTILE = 2
RING = (0, -1, 1, 2)
MESH = pl.DeviceIdType.MESH


def slot_at(table, n):
    return jnp.clip(table[0, n], 0, 127)


def key_slab(b, table, kbuf, kslab):
    first = kbuf[slot_at(table, b * WIN + WIN - 1)][0:1, :].astype(jnp.float32)
    first = jnp.broadcast_to(first, (ROWS, HD)).astype(jnp.bfloat16)
    for k in range(WIN):
        seen = jnp.full((ROWS, HD), table[1, b * WIN + k].astype(jnp.float32))
        unseen = (1.0 - seen).astype(jnp.bfloat16)
        keys = kbuf[slot_at(table, b * WIN + k)] * seen.astype(jnp.bfloat16) + first * unseen
        kslab[k * ROWS : (k + 1) * ROWS, 0:HD] = keys
        kslab[k * ROWS : (k + 1) * ROWS, HD : 2 * HD] = keys


def value_slab(b, table, vbuf, vslab):
    for k in range(WIN):
        seen = jnp.full((ROWS, HD), table[1, b * WIN + k].astype(jnp.float32)).astype(jnp.bfloat16)
        vslab[k * ROWS : (k + 1) * ROWS, 0:HD] = vbuf[slot_at(table, b * WIN + k)] * seen
        vslab[k * ROWS : (k + 1) * ROWS, HD : 2 * HD] = seen


def scores(b, j, qbuf, kslab, weights):
    row = lax.broadcasted_iota(jnp.int32, (ROWS, ROWS), 0)
    col = lax.broadcasted_iota(jnp.int32, (ROWS, ROWS), 1)
    causal = jnp.concatenate([col <= row] * TILE, 0)
    for t in range(GROUP // 2 // TILE):
        first = (j * (GROUP // 2) + t * TILE) * HD
        q = qbuf[b, :, first : first + TILE * HD]
        q = jnp.concatenate([q[:, i * HD : (i + 1) * HD] for i in range(TILE)], 0)
        q = q.astype(jnp.float32) * (LOG2E / math.sqrt(HD))
        high = q.astype(jnp.bfloat16)
        low = (q - high.astype(jnp.float32)).astype(jnp.bfloat16)
        s = lax.dot_general(
            jnp.concatenate([high, low], 1), kslab[...], (((1,), (1,)), ((), ())),
            preferred_element_type=jnp.float32,
        )
        edge = (WIN - 1) * ROWS
        s = jnp.concatenate([s[:, :edge], jnp.where(causal, s[:, edge:], -1e30)], 1)
        peak = jnp.max(s, axis=1, keepdims=True)
        weights[t * TILE * ROWS : (t + 1) * TILE * ROWS, :] = jnp.exp2(s - peak).astype(jnp.bfloat16)


def sums(b, j, weights, vslab, obuf):
    for t in range(GROUP // 2 // VTILE):
        o = jnp.dot(weights[t * VTILE * ROWS : (t + 1) * VTILE * ROWS, :], vslab[...], preferred_element_type=jnp.float32)
        r = (o[:, :HD] / o[:, HD:]).astype(jnp.bfloat16)
        for i in range(VTILE):
            first = (j * (GROUP // 2) + t * VTILE + i) * HD
            obuf[b, :, first : first + HD] = r[i * ROWS : (i + 1) * ROWS]


def kernel(order_hbm, window_hbm, row_hbm, q_ref, k_ref, v_ref, o_ref, qbuf, kbuf, vbuf, obuf, weights0, weights1, kslab, vslab, lookup, table, order_ref, window_ref, row_ref,
           a_send, a_recv, g_send, g_recv, o_send, o_recv, local):
    x = lax.axis_index("head")
    outer = lax.axis_index("outer")
    zh = lax.axis_index("inner")
    y, zl, c = outer // 4, (outer // 2) % 2, outer % 2

    def dev(dx=0, dy=0, dz=0, dc=0):
        yy = (y + dy + 4) % 4
        zz = (zh * 2 + zl + dz + 8) % 8
        cc = (c + dc) % 2
        return {"head": (x + dx + 4) % 4, "outer": yy * 4 + zz % 2 * 2 + cc, "inner": zz // 2}

    def slot(dy=0, dzh=0, dc=0):
        return ((((y + dy + 4) % 4) * 4 + (zh + dzh + 4) % 4) * 2 + (c + dc) % 2) * 4

    small = [pltpu.make_async_copy(src, dst, local.at[6 + n]) for n, (src, dst) in enumerate(
        ((order_hbm, order_ref), (window_hbm, window_ref), (row_hbm, row_ref)))]
    for copy in small:
        copy.start()
    barrier = pltpu.get_barrier_semaphore()
    partners = [dev(dx=dx, dz=dz) for dz in (0, 1, -1) for dx in range(4) if dx or dz]
    partners += [dev(dz=2), dev(dz=-2), dev(dy=1), dev(dy=-1), dev(dc=1)]
    for partner in partners:
        pl.semaphore_signal(barrier, inc=1, device_id=partner, device_id_type=MESH)
    pl.semaphore_wait(barrier, len(partners))

    sent = []

    def exchange(src, width, dst, send, recv, here):
        arriving = []
        for n, (dx, i) in enumerate((dx, i) for i in (None, 0, 1) for dx in range(4)):
            other, dz = (0, 0) if i is None else (1, 1 - 2 * i)
            take = slice(0, 2) if i is None else slice(i, i + 1)
            item, count = (0, 2) if i is None else (2 + i, 1)
            lanes = pl.ds(pl.multiple_of(((x + dx) % 4 * 2 + (zl + other) % 2) * width, width), width)
            if n == 0:
                copy = pltpu.make_async_copy(src.at[take, :, lanes], dst(own, item, count, x), here)
                copy.start()
                arriving.append(copy.wait)
            else:
                there_own = ((y * 4 + (zh * 2 + zl + dz + 8) % 8 // 2) * 2 + c) * 4
                there = dict(device_id=dev(dx=dx, dz=dz), device_id_type=MESH)
                copy = pltpu.make_async_remote_copy(
                    src.at[take, :, lanes], dst(there_own, item, count, x), send.at[n], recv.at[n], **there)
                copy.start()
                sent.append(copy)
                back = pltpu.make_async_remote_copy(
                    src.at[take, :, lanes], dst(own, item, count, (x - dx + 4) % 4), send.at[n], recv.at[n], **there)
                arriving.append(back.wait_recv)
        return arriving

    own = slot()
    arriving = []
    bufs = (kbuf, vbuf)
    for which, src, buf in ((0, k_ref, kbuf), (1, v_ref, vbuf)):
        arriving += exchange(
            src, HD,
            lambda base, item, count, xx, buf=buf: buf.at[pl.ds(base + item, count), pl.ds(32 * xx, 32), :],
            a_send.at[which], a_recv.at[which], local.at[which])
    for copy in small:
        copy.wait()
    lane = lax.broadcasted_iota(jnp.int32, (1, ROWS), 1)
    block = jnp.zeros((1, ROWS), jnp.int32)
    for b in range(4):
        zz = (zh * 2 + zl + (0, 0, 7, 1)[b]) % 8
        stored = ((y * 4 + zz % 2 * 2 + c) * 4 + zz // 2) * 2 + b % 2
        block = jnp.where(lane // WIN == b, order_ref[stored], block)
    back = WIN - 1 - lane % WIN
    wanted = block - back
    j = lax.broadcasted_iota(jnp.int32, (ROWS, ROWS), 0)
    moved = (j // 16 + zl) % 2
    zz = ((j // 2) % 4 * 2 + (j // 16) % 2 + moved * (1 - j % 2 * 2) + 8) % 8
    slots = (((j // 32) * 4 + zz // 2) * 2 + (j // 8) % 2) * 4 + moved * 2 + j % 2
    order = jnp.broadcast_to(row_ref[...], (ROWS, ROWS)).T
    lookup[0:1, :] = jnp.sum(jnp.where(order == wanted, slots, 0), axis=0, keepdims=True)
    lookup[1:2, :] = ((wanted >= 0) & (back < window_ref[x * 2 + zl])).astype(jnp.int32)
    lookup[2:8, :] = jnp.zeros((6, ROWS), jnp.int32)
    listing = pltpu.make_async_copy(lookup, table, local.at[5])
    listing.start()
    for wait in arriving[:12]:
        wait()

    names = {}

    def copy_of(name, w, first, count, device):
        n = names.setdefault((name, w), len(names))
        part = bufs[w].at[pl.ds(first, count)]
        return pltpu.make_async_remote_copy(
            part, part, g_send.at[n], g_recv.at[n], device_id=device, device_id_type=MESH)

    def send(name, w, first, count, device):
        copy = copy_of(name, w, first, count, device)
        copy.start()
        sent.append(copy)

    def arrived(name, w, first, count):
        copy_of(name, w, first, count, dev(dc=1)).wait_recv()

    pending = ([], [])

    def share(w, dy, dzh, half=None):
        off, count = (0, 4) if half is None else (2 * half, 2)
        name = ("c", dy, dzh, half)
        send(name, w, slot(dy, dzh) + off, count, dev(dc=1))
        pending[w].append((name, w, slot(dy, dzh, 1) + off, count))

    def to_z(w):
        send("z+", w, slot(), 4, dev(dz=2))
        send("z-", w, slot(), 4, dev(dz=-2))

    def from_z(w, r):
        arrived("z+" if r < 0 else "z-", w, slot(0, r), 4)
        half = 0 if r < 0 else 2
        send(("zz", r), w, slot(0, r) + half, 2, dev(dz=-2 * r))

    def from_zz(w):
        arrived(("zz", -1), w, slot(0, 2), 2)
        arrived(("zz", 1), w, slot(0, 2) + 2, 2)

    def to_y(w, r):
        send(("y+", r), w, slot(0, r), 4, dev(dy=1))
        send(("y-", r), w, slot(0, r), 4, dev(dy=-1))

    def from_y(w, r):
        arrived(("y+", r), w, slot(-1, r), 4)
        send(("yy+", r), w, slot(-1, r), 2, dev(dy=1))
        arrived(("y-", r), w, slot(1, r), 4)
        send(("yy-", r), w, slot(1, r) + 2, 2, dev(dy=-1))

    def share_y(w, r):
        share(w, -1, r)
        share(w, 1, r)

    def opposite(w, r):
        arrived(("yy+", r), w, slot(2, r), 2)
        share(w, 2, r, 0)
        arrived(("yy-", r), w, slot(2, r) + 2, 2)
        share(w, 2, r, 1)

    def to_zy(w, r):
        send(("zy", r), w, slot(r, r), 4, dev(dz=-2 * r))

    def from_zy(w):
        arrived(("zy", -1), w, slot(-1, 2), 4)
        send(("yy+", 2), w, slot(-1, 2), 2, dev(dy=1))
        arrived(("zy", 1), w, slot(1, 2), 4)
        send(("yy-", 2), w, slot(1, 2) + 2, 2, dev(dy=-1))

    K, V = 0, 1
    to_z(K)
    to_y(K, 0)
    for wait in arriving[12:]:
        wait()
    to_z(V)
    to_y(V, 0)
    share(K, 0, 0)
    share(V, 0, 0)
    from_y(K, 0)
    from_z(K, -1)
    to_y(K, -1)
    from_z(K, 1)
    to_y(K, 1)
    from_y(V, 0)
    share(K, 0, -1)
    share(K, 0, 1)
    share_y(K, 0)
    from_z(V, -1)
    to_y(V, -1)
    from_z(V, 1)
    to_y(V, 1)
    from_zz(K)
    from_y(K, -1)
    to_zy(K, -1)
    from_y(K, 1)
    to_zy(K, 1)
    queries_in = exchange(
        q_ref, GROUP * HD,
        lambda base, item, count, xx: qbuf.at[pl.ds(item, count), pl.ds(32 * xx, 32), :],
        a_send.at[2], a_recv.at[2], local.at[2])
    share(K, 0, 2)
    share_y(K, -1)
    share_y(K, 1)
    from_zz(V)
    to_y(V, 2)
    opposite(K, 0)
    from_zy(K)
    share_y(K, 2)
    for r in (-1, 1, 2):
        share(V, 0, r)
    share_y(V, 0)
    from_y(V, -1)
    from_y(V, 1)
    from_y(V, 2)
    for r in (-1, 1, 2):
        opposite(K, r)
    share_y(V, -1)
    share_y(V, 1)
    opposite(V, 0)
    share_y(V, 2)
    opposite(V, -1)
    opposite(V, 1)
    opposite(V, 2)
    listing.wait()
    for wait in queries_in:
        wait()
    for item in pending[K]:
        arrived(*item)
    width = GROUP * HD // 2

    def returns(b, j, start):
        other, i = b // 2, b % 2
        part = slice(j * width, (j + 1) * width)

        def copy_to(dx, xx, ll):
            lanes = pl.ds(pl.multiple_of((xx * 2 + ll) * 2 * width + j * width, width), width)
            return pltpu.make_async_remote_copy(
                obuf.at[b, pl.ds(32 * ((x + dx) % 4), 32), part], o_ref.at[i, :, lanes],
                o_send.at[b, dx, j], o_recv.at[b, dx, j], device_id=dev(dx=dx, dz=other * (2 * b - 5)), device_id_type=MESH)

        def remote(dx):
            if start:
                copy_to(dx, x, zl).start()
            else:
                copy_to(dx, x, zl).wait_send()
                copy_to(dx, (x - dx + 4) % 4, (zl + other) % 2).wait_recv()

        def here():
            lanes = pl.ds(pl.multiple_of((x * 2 + zl) * 2 * width + j * width, width), width)
            copy = pltpu.make_async_copy(
                obuf.at[b, pl.ds(32 * x, 32), part], o_ref.at[i, :, lanes], local.at[9 + 2 * i + j])
            copy.start() if start else copy.wait()

        for dx in (2, 1, 3):
            remote(dx)
        pl.when(other == 1)(lambda: remote(0))
        pl.when(other == 0)(here)

    def attend(n, last):
        b, after = (n + 2) % 4, (n + 3) % 4
        value_slab(b, table, vbuf, vslab)
        sums(b, 0, weights0, vslab, obuf)
        scores(b, 1, qbuf, kslab, weights1)
        returns(b, 0, True)
        sums(b, 1, weights1, vslab, obuf)
        if not last:
            key_slab(after, table, kbuf, kslab)
            scores(after, 0, qbuf, kslab, weights0)
        returns(b, 1, True)

    def attend_step(n, carry):
        attend(n, False)
        return carry

    def return_step(n, carry):
        returns((n + 2) % 4, 0, False)
        returns((n + 2) % 4, 1, False)
        return carry

    key_slab(2, table, kbuf, kslab)
    scores(2, 0, qbuf, kslab, weights0)
    for item in pending[V]:
        arrived(*item)
    lax.fori_loop(0, 3, attend_step, 0)
    attend(jnp.int32(3), True)
    for copy in sent:
        copy.wait_send()
    lax.fori_loop(0, 4, return_step, 0)


def body(queries, keys, values, half_order, window):
    hbm = pl.BlockSpec(memory_space=pltpu.HBM)
    dma = pltpu.SemaphoreType.DMA
    return pl.pallas_call(
        kernel,
        out_shape=jax.ShapeDtypeStruct(queries.shape, jnp.bfloat16),
        in_specs=[hbm] * 6,
        out_specs=hbm,
        scratch_shapes=[
            pltpu.VMEM((4, ROWS, GROUP * HD), jnp.bfloat16),
            pltpu.VMEM((128, ROWS, HD), jnp.bfloat16),
            pltpu.VMEM((128, ROWS, HD), jnp.bfloat16),
            pltpu.VMEM((4, ROWS, GROUP * HD), jnp.bfloat16),
            pltpu.VMEM((GROUP // 2 * ROWS, WIN * ROWS), jnp.bfloat16),
            pltpu.VMEM((GROUP // 2 * ROWS, WIN * ROWS), jnp.bfloat16),
            pltpu.VMEM((WIN * ROWS, 2 * HD), jnp.bfloat16),
            pltpu.VMEM((WIN * ROWS, 2 * HD), jnp.bfloat16),
            pltpu.VMEM((8, ROWS), jnp.int32),
            pltpu.SMEM((8, ROWS), jnp.int32),
            pltpu.SMEM((ROWS,), jnp.int32),
            pltpu.SMEM((8,), jnp.int32),
            pltpu.VMEM((1, ROWS), jnp.int32),
            dma((3, 12)), dma((3, 12)),
            dma((80,)), dma((80,)),
            dma((4, 4, 2)), dma((4, 4, 2)),
            dma((13,)),
        ],
        compiler_params=pltpu.CompilerParams(
            collective_id=0, has_side_effects=True, vmem_limit_bytes=60 * 1024 * 1024),
    )(half_order, window, half_order.reshape(1, ROWS), queries, keys, values)


def solution(mesh):
    rows = P(("outer", "inner"), "head", None)
    return jax.shard_map(
        body,
        mesh=mesh,
        in_specs=(rows, rows, rows, P(), P()),
        out_specs=rows,
        check_vma=False,
    )
```

```python
import math

import jax
import jax.numpy as jnp
from jax import lax
from jax.experimental import pallas as pl
from jax.experimental.pallas import tpu as pltpu
from jax.sharding import PartitionSpec as P

HD = 128
WIN = 16
ROWS = 128
GROUP = 8
LOG2E = 1.4426950408889634
TILE = 2
VTILE = 2
RING = (0, -1, 1, 2)
MESH = pl.DeviceIdType.MESH


def slot_at(table, n):
    return jnp.clip(table[0, n], 0, 127)


def key_slab(b, table, kbuf, kslab):
    first = kbuf[slot_at(table, b * WIN + WIN - 1)][0:1, :].astype(jnp.float32)
    first = jnp.broadcast_to(first, (ROWS, HD)).astype(jnp.bfloat16)
    for k in range(WIN):
        seen = jnp.full((ROWS, HD), table[1, b * WIN + k].astype(jnp.float32))
        unseen = (1.0 - seen).astype(jnp.bfloat16)
        keys = kbuf[slot_at(table, b * WIN + k)] * seen.astype(jnp.bfloat16) + first * unseen
        kslab[k * ROWS : (k + 1) * ROWS, 0:HD] = keys
        kslab[k * ROWS : (k + 1) * ROWS, HD : 2 * HD] = keys


def value_slab(b, table, vbuf, vslab):
    for k in range(WIN):
        seen = jnp.full((ROWS, HD), table[1, b * WIN + k].astype(jnp.float32)).astype(jnp.bfloat16)
        vslab[k * ROWS : (k + 1) * ROWS, 0:HD] = vbuf[slot_at(table, b * WIN + k)] * seen
        vslab[k * ROWS : (k + 1) * ROWS, HD : 2 * HD] = seen


def scores(b, j, qbuf, kslab, weights):
    row = lax.broadcasted_iota(jnp.int32, (ROWS, ROWS), 0)
    col = lax.broadcasted_iota(jnp.int32, (ROWS, ROWS), 1)
    causal = jnp.concatenate([col <= row] * TILE, 0)
    for t in range(GROUP // 2 // TILE):
        first = (j * (GROUP // 2) + t * TILE) * HD
        q = qbuf[b, :, first : first + TILE * HD]
        q = jnp.concatenate([q[:, i * HD : (i + 1) * HD] for i in range(TILE)], 0)
        q = q.astype(jnp.float32) * (LOG2E / math.sqrt(HD))
        high = q.astype(jnp.bfloat16)
        low = (q - high.astype(jnp.float32)).astype(jnp.bfloat16)
        s = lax.dot_general(
            jnp.concatenate([high, low], 1), kslab[...], (((1,), (1,)), ((), ())),
            preferred_element_type=jnp.float32,
        )
        edge = (WIN - 1) * ROWS
        s = jnp.concatenate([s[:, :edge], jnp.where(causal, s[:, edge:], -1e30)], 1)
        peak = jnp.max(s, axis=1, keepdims=True)
        weights[t * TILE * ROWS : (t + 1) * TILE * ROWS, :] = jnp.exp2(s - peak).astype(jnp.bfloat16)


def sums(b, j, weights, vslab, obuf):
    for t in range(GROUP // 2 // VTILE):
        o = jnp.dot(weights[t * VTILE * ROWS : (t + 1) * VTILE * ROWS, :], vslab[...], preferred_element_type=jnp.float32)
        r = (o[:, :HD] / o[:, HD:]).astype(jnp.bfloat16)
        for i in range(VTILE):
            first = (j * (GROUP // 2) + t * VTILE + i) * HD
            obuf[b, :, first : first + HD] = r[i * ROWS : (i + 1) * ROWS]


def kernel(order_hbm, window_hbm, row_hbm, q_ref, k_ref, v_ref, o_ref, qbuf, kbuf, vbuf, obuf, weights0, weights1, kslab, vslab, lookup, table, order_ref, window_ref, row_ref,
           a_send, a_recv, g_send, g_recv, o_send, o_recv, local):
    x = lax.axis_index("head")
    outer = lax.axis_index("outer")
    zh = lax.axis_index("inner")
    y, zl, c = outer // 4, (outer // 2) % 2, outer % 2

    def dev(dx=0, dy=0, dz=0, dc=0):
        yy = (y + dy + 4) % 4
        zz = (zh * 2 + zl + dz + 8) % 8
        cc = (c + dc) % 2
        return {"head": (x + dx + 4) % 4, "outer": yy * 4 + zz % 2 * 2 + cc, "inner": zz // 2}

    def slot(dy=0, dzh=0, dc=0):
        return ((((y + dy + 4) % 4) * 4 + (zh + dzh + 4) % 4) * 2 + (c + dc) % 2) * 4

    small = [pltpu.make_async_copy(src, dst, local.at[6 + n]) for n, (src, dst) in enumerate(
        ((order_hbm, order_ref), (window_hbm, window_ref), (row_hbm, row_ref)))]
    for copy in small:
        copy.start()
    barrier = pltpu.get_barrier_semaphore()
    partners = [dev(dx=dx, dz=dz) for dz in (0, 1, -1) for dx in range(4) if dx or dz]
    partners += [dev(dz=2), dev(dz=-2), dev(dy=1), dev(dy=-1), dev(dc=1)]
    for partner in partners:
        pl.semaphore_signal(barrier, inc=1, device_id=partner, device_id_type=MESH)
    pl.semaphore_wait(barrier, len(partners))

    sent = []

    def exchange(src, width, dst, send, recv, here):
        arriving = []
        for n, (dx, i) in enumerate((dx, i) for i in (None, 0, 1) for dx in range(4)):
            other, dz = (0, 0) if i is None else (1, 1 - 2 * i)
            take = slice(0, 2) if i is None else slice(i, i + 1)
            item, count = (0, 2) if i is None else (2 + i, 1)
            lanes = pl.ds(pl.multiple_of(((x + dx) % 4 * 2 + (zl + other) % 2) * width, width), width)
            if n == 0:
                copy = pltpu.make_async_copy(src.at[take, :, lanes], dst(own, item, count, x), here)
                copy.start()
                arriving.append(copy.wait)
            else:
                there_own = ((y * 4 + (zh * 2 + zl + dz + 8) % 8 // 2) * 2 + c) * 4
                there = dict(device_id=dev(dx=dx, dz=dz), device_id_type=MESH)
                copy = pltpu.make_async_remote_copy(
                    src.at[take, :, lanes], dst(there_own, item, count, x), send.at[n], recv.at[n], **there)
                copy.start()
                sent.append(copy)
                back = pltpu.make_async_remote_copy(
                    src.at[take, :, lanes], dst(own, item, count, (x - dx + 4) % 4), send.at[n], recv.at[n], **there)
                arriving.append(back.wait_recv)
        return arriving

    own = slot()
    arriving = []
    bufs = (kbuf, vbuf)
    for which, src, buf in ((0, k_ref, kbuf), (1, v_ref, vbuf)):
        arriving += exchange(
            src, HD,
            lambda base, item, count, xx, buf=buf: buf.at[pl.ds(base + item, count), pl.ds(32 * xx, 32), :],
            a_send.at[which], a_recv.at[which], local.at[which])
    for copy in small:
        copy.wait()
    lane = lax.broadcasted_iota(jnp.int32, (1, ROWS), 1)
    block = jnp.zeros((1, ROWS), jnp.int32)
    for b in range(4):
        zz = (zh * 2 + zl + (0, 0, 7, 1)[b]) % 8
        stored = ((y * 4 + zz % 2 * 2 + c) * 4 + zz // 2) * 2 + b % 2
        block = jnp.where(lane // WIN == b, order_ref[stored], block)
    back = WIN - 1 - lane % WIN
    wanted = block - back
    j = lax.broadcasted_iota(jnp.int32, (ROWS, ROWS), 0)
    moved = (j // 16 + zl) % 2
    zz = ((j // 2) % 4 * 2 + (j // 16) % 2 + moved * (1 - j % 2 * 2) + 8) % 8
    slots = (((j // 32) * 4 + zz // 2) * 2 + (j // 8) % 2) * 4 + moved * 2 + j % 2
    order = jnp.broadcast_to(row_ref[...], (ROWS, ROWS)).T
    lookup[0:1, :] = jnp.sum(jnp.where(order == wanted, slots, 0), axis=0, keepdims=True)
    lookup[1:2, :] = ((wanted >= 0) & (back < window_ref[x * 2 + zl])).astype(jnp.int32)
    lookup[2:8, :] = jnp.zeros((6, ROWS), jnp.int32)
    listing = pltpu.make_async_copy(lookup, table, local.at[5])
    listing.start()
    for wait in arriving[:12]:
        wait()

    names = {}

    def copy_of(name, w, first, count, device):
        n = names.setdefault((name, w), len(names))
        part = bufs[w].at[pl.ds(first, count)]
        return pltpu.make_async_remote_copy(
            part, part, g_send.at[n], g_recv.at[n], device_id=device, device_id_type=MESH)

    def send(name, w, first, count, device):
        copy = copy_of(name, w, first, count, device)
        copy.start()
        sent.append(copy)

    def arrived(name, w, first, count):
        copy_of(name, w, first, count, dev(dc=1)).wait_recv()

    pending = ([], [])

    def share(w, dy, dzh, half=None):
        off, count = (0, 4) if half is None else (2 * half, 2)
        name = ("c", dy, dzh, half)
        send(name, w, slot(dy, dzh) + off, count, dev(dc=1))
        pending[w].append((name, w, slot(dy, dzh, 1) + off, count))

    def to_z(w):
        send("z+", w, slot(), 4, dev(dz=2))
        send("z-", w, slot(), 4, dev(dz=-2))

    def from_z(w, r):
        arrived("z+" if r < 0 else "z-", w, slot(0, r), 4)
        half = 0 if r < 0 else 2
        send(("zz", r), w, slot(0, r) + half, 2, dev(dz=-2 * r))

    def from_zz(w):
        arrived(("zz", -1), w, slot(0, 2), 2)
        arrived(("zz", 1), w, slot(0, 2) + 2, 2)

    def to_y(w, r):
        send(("y+", r), w, slot(0, r), 4, dev(dy=1))
        send(("y-", r), w, slot(0, r), 4, dev(dy=-1))

    def from_y(w, r):
        arrived(("y+", r), w, slot(-1, r), 4)
        send(("yy+", r), w, slot(-1, r), 2, dev(dy=1))
        arrived(("y-", r), w, slot(1, r), 4)
        send(("yy-", r), w, slot(1, r) + 2, 2, dev(dy=-1))

    def share_y(w, r):
        share(w, -1, r)
        share(w, 1, r)

    def opposite(w, r):
        arrived(("yy+", r), w, slot(2, r), 2)
        share(w, 2, r, 0)
        arrived(("yy-", r), w, slot(2, r) + 2, 2)
        share(w, 2, r, 1)

    def to_zy(w, r):
        send(("zy", r), w, slot(r, r), 4, dev(dz=-2 * r))

    def from_zy(w):
        arrived(("zy", -1), w, slot(-1, 2), 4)
        send(("yy+", 2), w, slot(-1, 2), 2, dev(dy=1))
        arrived(("zy", 1), w, slot(1, 2), 4)
        send(("yy-", 2), w, slot(1, 2) + 2, 2, dev(dy=-1))

    K, V = 0, 1
    to_z(K)
    to_y(K, 0)
    for wait in arriving[12:]:
        wait()
    to_z(V)
    to_y(V, 0)
    share(K, 0, 0)
    share(V, 0, 0)
    from_y(K, 0)
    from_z(K, -1)
    to_y(K, -1)
    from_z(K, 1)
    to_y(K, 1)
    from_y(V, 0)
    share(K, 0, -1)
    share(K, 0, 1)
    share_y(K, 0)
    from_z(V, -1)
    to_y(V, -1)
    from_z(V, 1)
    to_y(V, 1)
    from_zz(K)
    from_y(K, -1)
    to_zy(K, -1)
    from_y(K, 1)
    to_zy(K, 1)
    share(K, 0, 2)
    share_y(K, -1)
    share_y(K, 1)
    from_zz(V)
    to_y(V, 2)
    queries_in = exchange(
        q_ref, GROUP * HD,
        lambda base, item, count, xx: qbuf.at[pl.ds(item, count), pl.ds(32 * xx, 32), :],
        a_send.at[2], a_recv.at[2], local.at[2])
    opposite(K, 0)
    from_zy(K)
    share_y(K, 2)
    for r in (-1, 1, 2):
        share(V, 0, r)
    share_y(V, 0)
    from_y(V, -1)
    from_y(V, 1)
    from_y(V, 2)
    for r in (-1, 1, 2):
        opposite(K, r)
    share_y(V, -1)
    share_y(V, 1)
    opposite(V, 0)
    share_y(V, 2)
    opposite(V, -1)
    opposite(V, 1)
    opposite(V, 2)
    listing.wait()
    for wait in queries_in:
        wait()
    for item in pending[K]:
        arrived(*item)
    width = GROUP * HD // 2

    def returns(b, j, start):
        other, i = b // 2, b % 2
        part = slice(j * width, (j + 1) * width)

        def copy_to(dx, xx, ll):
            lanes = pl.ds(pl.multiple_of((xx * 2 + ll) * 2 * width + j * width, width), width)
            return pltpu.make_async_remote_copy(
                obuf.at[b, pl.ds(32 * ((x + dx) % 4), 32), part], o_ref.at[i, :, lanes],
                o_send.at[b, dx, j], o_recv.at[b, dx, j], device_id=dev(dx=dx, dz=other * (2 * b - 5)), device_id_type=MESH)

        def remote(dx):
            if start:
                copy_to(dx, x, zl).start()
            else:
                copy_to(dx, x, zl).wait_send()
                copy_to(dx, (x - dx + 4) % 4, (zl + other) % 2).wait_recv()

        def here():
            lanes = pl.ds(pl.multiple_of((x * 2 + zl) * 2 * width + j * width, width), width)
            copy = pltpu.make_async_copy(
                obuf.at[b, pl.ds(32 * x, 32), part], o_ref.at[i, :, lanes], local.at[9 + 2 * i + j])
            copy.start() if start else copy.wait()

        for dx in (1, 3, 2):
            remote(dx)
        pl.when(other == 1)(lambda: remote(0))
        pl.when(other == 0)(here)

    def attend(n, last):
        b, after = (n + 2) % 4, (n + 3) % 4
        value_slab(b, table, vbuf, vslab)
        sums(b, 0, weights0, vslab, obuf)
        scores(b, 1, qbuf, kslab, weights1)
        returns(b, 0, True)
        sums(b, 1, weights1, vslab, obuf)
        if not last:
            key_slab(after, table, kbuf, kslab)
            scores(after, 0, qbuf, kslab, weights0)
        returns(b, 1, True)

    def attend_step(n, carry):
        attend(n, False)
        return carry

    def return_step(n, carry):
        returns((n + 2) % 4, 0, False)
        returns((n + 2) % 4, 1, False)
        return carry

    key_slab(2, table, kbuf, kslab)
    scores(2, 0, qbuf, kslab, weights0)
    for item in pending[V]:
        arrived(*item)
    lax.fori_loop(0, 3, attend_step, 0)
    attend(jnp.int32(3), True)
    for copy in sent:
        copy.wait_send()
    lax.fori_loop(0, 4, return_step, 0)


def body(queries, keys, values, half_order, window):
    hbm = pl.BlockSpec(memory_space=pltpu.HBM)
    dma = pltpu.SemaphoreType.DMA
    return pl.pallas_call(
        kernel,
        out_shape=jax.ShapeDtypeStruct(queries.shape, jnp.bfloat16),
        in_specs=[hbm] * 6,
        out_specs=pl.BlockSpec(memory_space=pl.ANY),
        scratch_shapes=[
            pltpu.VMEM((4, ROWS, GROUP * HD), jnp.bfloat16),
            pltpu.VMEM((128, ROWS, HD), jnp.bfloat16),
            pltpu.VMEM((128, ROWS, HD), jnp.bfloat16),
            pltpu.VMEM((4, ROWS, GROUP * HD), jnp.bfloat16),
            pltpu.VMEM((GROUP // 2 * ROWS, WIN * ROWS), jnp.bfloat16),
            pltpu.VMEM((GROUP // 2 * ROWS, WIN * ROWS), jnp.bfloat16),
            pltpu.VMEM((WIN * ROWS, 2 * HD), jnp.bfloat16),
            pltpu.VMEM((WIN * ROWS, 2 * HD), jnp.bfloat16),
            pltpu.VMEM((8, ROWS), jnp.int32),
            pltpu.SMEM((8, ROWS), jnp.int32),
            pltpu.SMEM((ROWS,), jnp.int32),
            pltpu.SMEM((8,), jnp.int32),
            pltpu.VMEM((1, ROWS), jnp.int32),
            dma((3, 12)), dma((3, 12)),
            dma((80,)), dma((80,)),
            dma((4, 4, 2)), dma((4, 4, 2)),
            dma((13,)),
        ],
        compiler_params=pltpu.CompilerParams(
            collective_id=0, has_side_effects=True, vmem_limit_bytes=44 * 1024 * 1024),
    )(*(pltpu.with_memory_space_constraint(v, pltpu.HBM) for v in (
        half_order, window, half_order.reshape(1, ROWS), queries, keys, values)))


def solution(mesh):
    rows = P(("outer", "inner"), "head", None)
    return jax.shard_map(
        body,
        mesh=mesh,
        in_specs=(rows, rows, rows, P(), P()),
        out_specs=rows,
        check_vma=False,
    )
```
